32 devices in a mesh: shard: 8 (over y, x, core), replica: 4 (over z).
Axes of the slice: x: 2, y: 2, z: 4, core: 2. Of those that a mesh axis runs over, the one named last changes fastest.
Arguments:
- grads: bfloat16 [4, 32, 256, 256], P('replica', None, 'shard')
- table: int32 [32], replicated, may hold values from 0 to 31, each once
- left_code: bfloat16 [32, 256, 256], P(('shard', 'replica')), may hold values from -7 to 7, as said below
- left_scale: float32 [32, 2, 256], P(('shard', 'replica')), may hold values from 0.2 to 2
- right_code: bfloat16 [32, 256, 256], P(('shard', 'replica')), may hold values from -7 to 7, as said below
- right_scale: float32 [32, 2, 256], P(('shard', 'replica')), may hold values from 0.2 to 2
- left_root_code: bfloat16 [32, 256, 256], P(('shard', 'replica')), may hold values from -7 to 7, as said below
- left_root_scale: float32 [32, 2, 256], P(('shard', 'replica')), may hold values from 0.01 to 0.1
- right_root_code: bfloat16 [32, 256, 256], P(('shard', 'replica')), may hold values from -7 to 7, as said below
- right_root_scale: float32 [32, 2, 256], P(('shard', 'replica')), may hold values from 0.01 to 0.1
Outputs:
- direction: bfloat16 [32, 256, 256], P(None, 'shard')
- new_left: bfloat16 [32, 256, 256], P(('shard', 'replica'))
- new_left_scale: float32 [32, 2, 256], P(('shard', 'replica'))
- new_right: bfloat16 [32, 256, 256], P(('shard', 'replica'))
- new_right_scale: float32 [32, 2, 256], P(('shard', 'replica'))
The draws below stay inside these ranges and needn't reach their ends.
Inputs may be any that keep to these rules, and one draw needn't show every extreme that they name: `table`: a permutation: every block is held by exactly one slot. `left_code`: whole numbers. `right_code`: whole numbers. `left_root_code`: whole numbers. `right_root_code`: whole numbers.
All inputs are finite; a program needn't handle non-finite values.
Results may differ from the reference program's by a relative error of at most 0.012.
Values may be sent and summed in bfloat16 or wider, within the bound.
A program may use at most 64 MiB of HBM per device.

```python
import math
import jax
import jax.numpy as jnp
from jax import lax

BS = 256
QG = 128
BLOCKS = 32
N_REPLICA = 4


def code_values(key):
    return jax.random.randint(key, (BLOCKS, BS, BS), -7, 8).astype(jnp.float32).astype(jnp.bfloat16)


def draw_grads(key, part):
    key = jax.random.fold_in(key, 11)
    key_rows = jax.random.fold_in(key, 0)
    key_cols = jax.random.fold_in(key, 1)
    key_own = jax.random.fold_in(key, 3)
    row_scale = jnp.exp(jax.random.uniform(key_rows, (BLOCKS, BS, 1), jnp.float32, math.log(0.1), 0.0))
    col_scale = jnp.exp(jax.random.uniform(key_cols, (BLOCKS, 1, BS), jnp.float32, math.log(0.1), 0.0))
    values = jax.random.normal(key_own, (N_REPLICA, BLOCKS, BS, BS), jnp.float32) * row_scale[None] * col_scale[None]
    return values.astype(jnp.bfloat16)


def draw_left_code(key, part):
    key = jax.random.fold_in(key, 21)
    return code_values(key)


def draw_right_code(key, part):
    key = jax.random.fold_in(key, 22)
    return code_values(key)


def draw_left_root_code(key, part):
    key = jax.random.fold_in(key, 23)
    return code_values(key)


def draw_right_root_code(key, part):
    key = jax.random.fold_in(key, 24)
    return code_values(key)


def level_of(stream_key, shape, cuts, smallest, top_value):
    loudness = 1.0
    for dim, parts in cuts:
        steps = jax.random.uniform(jax.random.fold_in(jax.random.fold_in(stream_key, 6), dim), (parts,), jnp.float32, smallest / len(cuts), top_value / len(cuts))
        loudness = loudness * jnp.repeat(jnp.exp(steps), shape[dim] // parts).reshape((-1,) + (1,) * (len(shape) - 1 - dim))
    return loudness


def setup_inputs(seed: int = 0) -> dict:
    streams_of = jax.random.split(jax.random.key(seed), 11)
    grads = draw_grads(jax.random.fold_in(streams_of[10], 71), 0)
    table = jax.random.permutation(streams_of[1], BLOCKS).astype(jnp.int32)
    left_code = draw_left_code(jax.random.fold_in(streams_of[10], 71), 0)
    left_scale = jnp.clip(jnp.exp(math.log(2.0) - 2.3025851 * jax.random.uniform(streams_of[3], (BLOCKS, BS // QG, BS), jnp.float32) ** level_of(streams_of[3], (BLOCKS, BS // QG, BS), ((0, 32),), -0.2, 0.2)), 0.2, 2.0)
    right_code = draw_right_code(jax.random.fold_in(streams_of[10], 71), 0)
    right_scale = jnp.clip(jnp.exp(math.log(2.0) - 2.3025851 * jax.random.uniform(streams_of[5], (BLOCKS, BS // QG, BS), jnp.float32) ** level_of(streams_of[5], (BLOCKS, BS // QG, BS), ((0, 32),), -0.2, 0.2)), 0.2, 2.0)
    left_root_code = draw_left_root_code(jax.random.fold_in(streams_of[10], 71), 0)
    left_root_scale = jnp.clip(jnp.exp(math.log(0.1) - 2.3025851 * jax.random.uniform(streams_of[7], (BLOCKS, BS // QG, BS), jnp.float32) ** level_of(streams_of[7], (BLOCKS, BS // QG, BS), ((0, 32),), -0.2, 0.2)), 0.01, 0.1)
    right_root_code = draw_right_root_code(jax.random.fold_in(streams_of[10], 71), 0)
    right_root_scale = jnp.clip(jnp.exp(math.log(0.1) - 2.3025851 * jax.random.uniform(streams_of[9], (BLOCKS, BS // QG, BS), jnp.float32) ** level_of(streams_of[9], (BLOCKS, BS // QG, BS), ((0, 32),), -0.2, 0.2)), 0.01, 0.1)
    return dict(grads=grads, table=table, left_code=left_code, left_scale=left_scale, right_code=right_code, right_scale=right_scale, left_root_code=left_root_code, left_root_scale=left_root_scale, right_root_code=right_root_code, right_root_scale=right_root_scale)


DECAY = 0.9
EPSILON = 1e-06

def dequantize(code_block, scale_grid):
    grouped = code_block.astype(jnp.float32).reshape(BS, BS // QG, QG)
    return (grouped * scale_grid.T[:, :, None]).reshape(BS, BS)

def requantize(matrix):
    grouped = matrix.reshape(BS, BS // QG, QG)
    largest = lax.optimization_barrier(jnp.max(jnp.abs(grouped), axis=2))
    step_size = (largest + EPSILON) / 7.0
    values = (grouped / step_size[:, :, None]).reshape(BS, BS).astype(jnp.bfloat16)
    return (values, step_size.T)

def reference(grads, table, left_code, left_scale, right_code, right_scale, left_root_code, left_root_scale, right_root_code, right_root_scale):
    highest = lax.Precision.HIGHEST

    def one_slot(slot_index):
        block_id = table[slot_index]
        summed = lax.optimization_barrier(jnp.sum(grads[:, block_id].astype(jnp.float32), axis=0))
        left = dequantize(left_code[slot_index], left_scale[slot_index])
        right = dequantize(right_code[slot_index], right_scale[slot_index])
        left_root = dequantize(left_root_code[slot_index], left_root_scale[slot_index])
        right_root = dequantize(right_root_code[slot_index], right_root_scale[slot_index])
        left_new = DECAY * left + (1.0 - DECAY) * jnp.dot(summed, summed.T, precision=highest)
        right_new = DECAY * right + (1.0 - DECAY) * jnp.dot(summed.T, summed, precision=highest)
        product = jnp.dot(jnp.dot(left_root, summed, precision=highest), right_root, precision=highest)
        ratio = jnp.sqrt(jnp.mean(summed * summed) + EPSILON) / jnp.sqrt(jnp.mean(product * product) + EPSILON)
        moved = (product * ratio).astype(jnp.bfloat16)
        left_values, left_steps = requantize(left_new)
        right_values, right_steps = requantize(right_new)
        return (moved, left_values, left_steps, right_values, right_steps)
    results = lax.map(one_slot, jnp.arange(BLOCKS, dtype=jnp.int32))
    direction = jnp.zeros((BLOCKS, BS, BS), jnp.bfloat16).at[table].set(results[0])
    return (direction, results[1], results[2], results[3], results[4])
```

```python
import functools

import jax
import jax.numpy as jnp
from jax import lax
from jax.experimental import pallas as pl
from jax.experimental.pallas import tpu as pltpu
from jax.sharding import PartitionSpec as P

QG = 128
DECAY = 0.9
EPSILON = 1e-06
MESH = pl.DeviceIdType.MESH
F32 = jnp.float32
BF16 = jnp.bfloat16


def kernel(
    shards,
    copies,
    table,
    grads_hbm,
    lc_hbm,
    ls_hbm,
    rc_hbm,
    rs_hbm,
    lrc_hbm,
    lrs_hbm,
    rrc_hbm,
    rrs_hbm,
    direction,
    new_left,
    new_left_scale,
    new_right,
    new_right_scale,
    grads,
    lc,
    ls,
    rc,
    rs,
    lrc,
    lrs,
    rrc,
    rrs,
    packed,
    arrived,
    part,
    full,
    moved,
    got,
    place,
    in_sem,
    a1_send,
    a1_recv,
    a2_send,
    a2_recv,
    b1_send,
    b1_recv,
    b2_send,
    b2_recv,
):
    me_s = lax.axis_index("shard")
    me_r = lax.axis_index("replica")
    rows = grads.shape[1]
    order = lc.shape[1]
    blocks = shards * copies

    loads = []
    for k, (src, dst) in enumerate(
        [
            (grads_hbm.at[0], grads),
            (lrc_hbm, lrc),
            (lrs_hbm, lrs),
            (rrc_hbm, rrc),
            (rrs_hbm, rrs),
            (lc_hbm, lc),
            (ls_hbm, ls),
            (rc_hbm, rc),
            (rs_hbm, rs),
        ]
    ):
        copy = pltpu.make_async_copy(src, dst, in_sem.at[k])
        copy.start()
        loads.append(copy)

    barrier = pltpu.get_barrier_semaphore()
    for d in range(1, copies):
        pl.semaphore_signal(
            barrier, inc=1, device_id=(me_s, lax.rem(me_r + d, copies)), device_id_type=MESH
        )
    for d in range(1, shards):
        pl.semaphore_signal(
            barrier, inc=1, device_id=(lax.rem(me_s + d, shards), me_r), device_id_type=MESH
        )

    loads[0].wait()

    def pack(k, carry):
        packed[k] = grads[table[lax.rem(k, shards) * copies + k // shards]]
        return carry

    lax.fori_loop(0, blocks, pack, 0, unroll=4)
    pl.semaphore_wait(barrier, copies - 1 + shards - 1)

    sends = []
    for d in range(1, copies):
        to = lax.rem(me_r + d, copies)
        copy = pltpu.make_async_remote_copy(
            src_ref=packed.at[pl.ds(to * shards, shards)],
            dst_ref=arrived.at[d - 1],
            send_sem=a1_send.at[d - 1],
            recv_sem=a1_recv.at[d - 1],
            device_id=(me_s, to),
            device_id_type=MESH,
        )
        copy.start()
        sends.append(copy)

    def locate(b, carry):
        def look(q, found):
            spot = lax.rem(q, copies) * shards + q // copies
            return jnp.where(table[q] == b, spot, found)

        place[b] = lax.fori_loop(0, blocks, look, jnp.int32(0), unroll=8)
        return carry

    lax.fori_loop(0, blocks, locate, 0)

    for copy in sends:
        copy.wait()
    total = packed[pl.ds(me_r * shards, shards)].astype(F32)
    for d in range(1, copies):
        total = total + arrived[d - 1].astype(F32)
    part[...] = total.astype(BF16)

    sends = []
    for d in range(1, shards):
        to = lax.rem(me_s + d, shards)
        copy = pltpu.make_async_remote_copy(
            src_ref=part.at[to],
            dst_ref=full.at[me_s],
            send_sem=a2_send.at[d - 1],
            recv_sem=a2_recv.at[d - 1],
            device_id=(to, me_r),
            device_id_type=MESH,
        )
        copy.start()
        sends.append(copy)
    full[me_s] = part[me_s]
    for copy in loads[1:]:
        copy.wait()
    zeros = jnp.zeros((2, order), F32)
    columns = jnp.concatenate([ls[0], rs[0], lrs[0], zeros], axis=0).T
    for copy in sends:
        copy.wait()

    summed32 = full[...].astype(F32).reshape(order, order)
    summed = summed32.astype(BF16)
    half = columns[:, 4:5] * jnp.dot(lrc[0, :, :QG], summed[:QG], preferred_element_type=F32)
    half = half + columns[:, 5:6] * jnp.dot(
        lrc[0, :, QG:], summed[QG:], preferred_element_type=F32
    )
    product = jnp.concatenate(
        [
            jnp.dot(
                (half * rrs[0, g : g + 1]).astype(BF16),
                rrc[0, :, g * QG : (g + 1) * QG],
                preferred_element_type=F32,
            )
            for g in range(order // QG)
        ],
        axis=1,
    )
    count = 1.0 / (order * order)
    grad_power = jnp.sum(jnp.sum(summed32 * summed32, axis=0, keepdims=True), axis=1, keepdims=True)
    prod_power = jnp.sum(jnp.sum(product * product, axis=0, keepdims=True), axis=1, keepdims=True)
    ratio = jnp.sqrt(grad_power * count + EPSILON) / jnp.sqrt(prod_power * count + EPSILON)
    moved[...] = (product * ratio).reshape(shards, rows, order).astype(BF16)

    mine = me_r * shards
    sends = []
    for d in range(1, shards):
        to = lax.rem(me_s + d, shards)
        copy = pltpu.make_async_remote_copy(
            src_ref=moved.at[to],
            dst_ref=got.at[mine + me_s],
            send_sem=b1_send.at[d - 1],
            recv_sem=b1_recv.at[d - 1],
            device_id=(to, me_r),
            device_id_type=MESH,
        )
        copy.start()
        sends.append(copy)
    got[mine + me_s] = moved[me_s]
    for copy in sends:
        copy.wait()

    sends = []
    for d in range(1, copies):
        to = lax.rem(me_r + d, copies)
        copy = pltpu.make_async_remote_copy(
            src_ref=got.at[pl.ds(mine, shards)],
            dst_ref=got.at[pl.ds(mine, shards)],
            send_sem=b2_send.at[d - 1],
            recv_sem=b2_recv.at[d - 1],
            device_id=(me_s, to),
            device_id_type=MESH,
        )
        copy.start()
        sends.append(copy)

    scales = []
    lane = lax.broadcasted_iota(jnp.int32, (order, QG), 1)
    table_of_scales = jnp.zeros((order, QG), F32)
    for k, (code, gram, out) in enumerate(
        [
            (
                lc,
                lax.dot_general(
                    summed, summed, (((1,), (1,)), ((), ())), preferred_element_type=F32
                ),
                new_left,
            ),
            (
                rc,
                lax.dot_general(
                    summed, summed, (((0,), (0,)), ((), ())), preferred_element_type=F32
                ),
                new_right,
            ),
        ]
    ):
        for g in range(order // QG):
            at = 2 * k + g
            cols = slice(g * QG, (g + 1) * QG)
            old = code[0, :, cols].astype(F32) * columns[:, at : at + 1]
            new = DECAY * old + (1.0 - DECAY) * gram[:, cols]
            step = (jnp.max(jnp.abs(new), axis=1, keepdims=True) + EPSILON) / 7.0
            out[0, :, cols] = (new * (1.0 / step)).astype(BF16)
            table_of_scales = jnp.where(lane == at, step, table_of_scales)
    flipped = table_of_scales.T
    new_left_scale[0] = flipped[0:2]
    new_right_scale[0] = flipped[2:4]

    for copy in sends:
        copy.wait()

    def put(b, carry):
        direction[b] = got[place[b]]
        return carry

    lax.fori_loop(0, blocks, put, 0, unroll=4)


def local(shards, copies, grads, table, *factors):
    blocks, rows, order = grads.shape[1:]
    vmem = pl.BlockSpec(memory_space=pltpu.VMEM)
    hbm = pl.BlockSpec(memory_space=pl.ANY)
    code = jax.ShapeDtypeStruct((1, order, order), BF16)
    scale = jax.ShapeDtypeStruct((1, order // QG, order), F32)
    dma = pltpu.SemaphoreType.DMA
    return pl.pallas_call(
        functools.partial(kernel, shards, copies),
        out_shape=[jax.ShapeDtypeStruct((blocks, rows, order), BF16), code, scale, code, scale],
        in_specs=[pl.BlockSpec(memory_space=pltpu.SMEM)] + [hbm] * 9,
        out_specs=[vmem] * 5,
        scratch_shapes=[pltpu.VMEM((blocks, rows, order), BF16)]
        + [pltpu.VMEM(f.shape, f.dtype) for f in factors]
        + [
            pltpu.VMEM((blocks, rows, order), BF16),
            pltpu.VMEM((copies - 1, shards, rows, order), BF16),
            pltpu.VMEM((shards, rows, order), BF16),
            pltpu.VMEM((shards, rows, order), BF16),
            pltpu.VMEM((shards, rows, order), BF16),
            pltpu.VMEM((blocks, rows, order), BF16),
            pltpu.SMEM((blocks,), jnp.int32),
            dma((9,)),
            dma((copies - 1,)),
            dma((copies - 1,)),
            dma((shards - 1,)),
            dma((shards - 1,)),
            dma((shards - 1,)),
            dma((shards - 1,)),
            dma((copies - 1,)),
            dma((copies - 1,)),
        ],
        compiler_params=pltpu.CompilerParams(
            collective_id=0, has_side_effects=True, vmem_limit_bytes=48 * 1024 * 1024
        ),
    )(table, grads, *factors)


def solution(mesh):
    slots = P(("shard", "replica"), None, None)
    return jax.shard_map(
        functools.partial(local, mesh.shape["shard"], mesh.shape["replica"]),
        mesh=mesh,
        in_specs=(P("replica", None, "shard", None), P()) + (slots,) * 8,
        out_specs=(P(None, "shard", None), slots, slots, slots, slots),
        check_vma=False,
    )
```

```python
import functools

import jax
import jax.numpy as jnp
from jax import lax
from jax.experimental import pallas as pl
from jax.experimental.pallas import tpu as pltpu
from jax.sharding import PartitionSpec as P

QG = 128
DECAY = 0.9
EPSILON = 1e-06
VMEM_BYTES = 64 * 1024 * 1024
MESH = pl.DeviceIdType.MESH
F32 = jnp.float32
BF16 = jnp.bfloat16


def kernel(
    shards,
    copies,
    cuts,
    table,
    grads_hbm,
    lc_hbm,
    ls_hbm,
    rc_hbm,
    rs_hbm,
    lrc_hbm,
    lrs_hbm,
    rrc_hbm,
    rrs_hbm,
    got,
    new_left,
    new_left_scale,
    new_right,
    new_right_scale,
    grads,
    lc,
    ls,
    rc,
    rs,
    lrc,
    lrs,
    rrc,
    rrs,
    packed,
    arrived,
    part,
    full,
    moved,
    in_sem,
    a1_send,
    a1_recv,
    a2_send,
    a2_recv,
    b1_send,
    b1_recv,
    b2_send,
    b2_recv,
):
    me_s = lax.axis_index("shard")
    me_r = lax.axis_index("replica")
    rows = grads.shape[1]
    order = lc.shape[1]
    blocks = shards * copies
    size = shards // cuts
    in_line = copies == 4

    loads = []
    for k, (src, dst) in enumerate(
        [
            (grads_hbm.at[0], grads),
            (lrc_hbm, lrc),
            (lrs_hbm, lrs),
            (rrc_hbm, rrc),
            (rrs_hbm, rrs),
            (lc_hbm, lc),
            (ls_hbm, ls),
            (rc_hbm, rc),
            (rs_hbm, rs),
        ]
    ):
        copy = pltpu.make_async_copy(src, dst, in_sem.at[k])
        copy.start()
        loads.append(copy)

    barrier = pltpu.get_barrier_semaphore()
    for d in range(1, copies):
        pl.semaphore_signal(
            barrier, inc=1, device_id=(me_s, lax.rem(me_r + d, copies)), device_id_type=MESH
        )
    for d in range(1, shards):
        pl.semaphore_signal(
            barrier, inc=1, device_id=(lax.rem(me_s + d, shards), me_r), device_id_type=MESH
        )

    loads[0].wait()

    def pack(k, carry):
        packed[k] = grads[table[lax.rem(k, shards) * copies + k // shards]]
        return carry

    lax.fori_loop(0, blocks, pack, 0, unroll=8)
    pl.semaphore_wait(barrier, copies - 1 + shards - 1)

    def group(r, c):
        return pl.ds(r * shards + c * size, size)

    def chunk(c):
        return pl.ds(c * size, size)

    partner = me_r + 1 - 2 * lax.rem(me_r, 2)
    opposite = copies - 1 - me_r
    across = copies - 1 - partner
    is_end = jnp.logical_or(me_r == 0, me_r == copies - 1)
    is_mid = jnp.logical_not(is_end)
    DIRECT, PAIR, RELAY = 0, 1, 2

    def a_copy(src, slot, c, k, to):
        return pltpu.make_async_remote_copy(
            src_ref=src,
            dst_ref=arrived.at[slot, chunk(c)],
            send_sem=a1_send.at[k, c],
            recv_sem=a1_recv.at[slot, c],
            device_id=(me_s, to),
            device_id_type=MESH,
        )

    def end_a(k, c):
        to_group = [across, partner, opposite][k]
        slot = [RELAY, DIRECT, RELAY + 1][k]
        return a_copy(packed.at[group(to_group, c)], slot, c, k, partner)

    def mid_direct(c):
        return a_copy(packed.at[group(partner, c)], DIRECT, c, 0, partner)

    def mid_relay(k, c):
        src = arrived.at[RELAY + k, chunk(c)]
        return a_copy(src, PAIR, c, 1 + k, [opposite, across][k])

    def relay(k):
        for c in range(cuts):
            a_copy(packed.at[chunk(c)], RELAY + k, c, 0, partner).wait_recv()
            own = packed[group([opposite, across][k], c)].astype(F32)
            arrived[RELAY + k, chunk(c)] = (
                arrived[RELAY + k, chunk(c)].astype(F32) + own
            ).astype(BF16)
            mid_relay(k, c).start()

    def far(d, c):
        to = lax.rem(me_r + d, copies)
        return a_copy(packed.at[group(to, c)], d - 1, c, d - 1, to)

    if in_line:

        @pl.when(is_end)
        def _():
            for k in range(3):
                for c in range(cuts):
                    end_a(k, c).start()

        @pl.when(is_mid)
        def _():
            for c in range(cuts):
                mid_direct(c).start()
            relay(0)

    else:
        for c in range(cuts):
            for d in range(1, copies):
                far(d, c).start()

    def a2_copy(to):
        return pltpu.make_async_remote_copy(
            src_ref=part.at[to],
            dst_ref=full.at[me_s],
            send_sem=a2_send.at[to],
            recv_sem=a2_recv.at[me_s],
            device_id=(to, me_r),
            device_id_type=MESH,
        )

    def a2_arrival(source):
        return pltpu.make_async_remote_copy(
            src_ref=part.at[source],
            dst_ref=full.at[source],
            send_sem=a2_send.at[source],
            recv_sem=a2_recv.at[source],
            device_id=(source, me_r),
            device_id_type=MESH,
        )

    for c in range(cuts):
        total = packed[group(me_r, c)].astype(F32)
        for slot in [DIRECT, PAIR] if in_line else range(copies - 1):
            a_copy(packed.at[chunk(c)], slot, c, 0, partner).wait_recv()
            total = total + arrived[slot, chunk(c)].astype(F32)
        part[chunk(c)] = total.astype(BF16)
        for k in range(size):
            to = c * size + lax.rem(me_s + k, size)

            @pl.when(to != me_s)
            def _():
                a2_copy(to).start()

    if in_line:

        @pl.when(is_mid)
        def _():
            relay(1)

    full[me_s] = part[me_s]
    for copy in loads[1:]:
        copy.wait()
    zeros = jnp.zeros((2, order), F32)
    columns = jnp.concatenate([ls[0], rs[0], lrs[0], zeros], axis=0).T
    for d in range(1, shards):
        a2_arrival(lax.rem(me_s + d, shards)).wait_recv()

    summed32 = full[...].astype(F32).reshape(order, order)
    summed = summed32.astype(BF16)
    half = columns[:, 4:5] * jnp.dot(lrc[0, :, :QG], summed[:QG], preferred_element_type=F32)
    half = half + columns[:, 5:6] * jnp.dot(
        lrc[0, :, QG:], summed[QG:], preferred_element_type=F32
    )
    product = jnp.concatenate(
        [
            jnp.dot(
                (half * rrs[0, g : g + 1]).astype(BF16),
                rrc[0, :, g * QG : (g + 1) * QG],
                preferred_element_type=F32,
            )
            for g in range(order // QG)
        ],
        axis=1,
    )
    count = 1.0 / (order * order)
    grad_power = jnp.sum(jnp.sum(summed32 * summed32, axis=0, keepdims=True), axis=1, keepdims=True)
    prod_power = jnp.sum(jnp.sum(product * product, axis=0, keepdims=True), axis=1, keepdims=True)
    ratio = jnp.sqrt(grad_power * count + EPSILON) / jnp.sqrt(prod_power * count + EPSILON)
    moved[...] = (product * ratio).reshape(shards, rows, order).astype(BF16)

    mine = me_r * shards

    def b1_copy(to):
        return pltpu.make_async_remote_copy(
            src_ref=moved.at[to],
            dst_ref=got.at[mine + me_s],
            send_sem=b1_send.at[to],
            recv_sem=b1_recv.at[me_s],
            device_id=(to, me_r),
            device_id_type=MESH,
        )

    def b1_arrival(source):
        return pltpu.make_async_remote_copy(
            src_ref=moved.at[source],
            dst_ref=got.at[mine + source],
            send_sem=b1_send.at[source],
            recv_sem=b1_recv.at[source],
            device_id=(source, me_r),
            device_id_type=MESH,
        )

    for d in range(1, shards):
        b1_copy(lax.rem(me_s + d, shards)).start()
    got[mine + me_s] = moved[me_s]

    lane = lax.broadcasted_iota(jnp.int32, (order, QG), 1)

    def statistic(k, code, contracted, out, steps):
        gram = lax.dot_general(
            summed, summed, (((contracted,), (contracted,)), ((), ())), preferred_element_type=F32
        )
        for g in range(order // QG):
            at = 2 * k + g
            cols = slice(g * QG, (g + 1) * QG)
            old = code[0, :, cols].astype(F32) * columns[:, at : at + 1]
            new = DECAY * old + (1.0 - DECAY) * gram[:, cols]
            step = (jnp.max(jnp.abs(new), axis=1, keepdims=True) + EPSILON) / 7.0
            out[0, :, cols] = (new * (1.0 / step)).astype(BF16)
            steps = jnp.where(lane == at, step, steps)
        return steps

    steps = statistic(0, lc, 1, new_left, jnp.zeros((order, QG), F32))

    def b_copy(r, c, k, to):
        return pltpu.make_async_remote_copy(
            src_ref=got.at[group(r, c)],
            dst_ref=got.at[group(r, c)],
            send_sem=b2_send.at[k, c],
            recv_sem=b2_recv.at[r, c],
            device_id=(me_s, to),
            device_id_type=MESH,
        )

    def own_sends(c):
        if not in_line:
            return [
                b_copy(me_r, c, d - 1, lax.rem(me_r + d, copies)) for d in range(1, copies)
            ]
        return [
            b_copy(me_r, c, 0, partner),
            b_copy(me_r, c, 1, jnp.where(is_end, across, opposite)),
        ]

    for c in range(cuts):
        for s in range(c * size, (c + 1) * size):

            @pl.when(s != me_s)
            def _():
                b1_arrival(s).wait_recv()

        for copy in own_sends(c):
            copy.start()

    steps = statistic(1, rc, 0, new_right, steps)
    flipped = steps.T
    new_left_scale[0] = flipped[0:2]
    new_right_scale[0] = flipped[2:4]

    if in_line:

        @pl.when(is_mid)
        def _():
            for k, r in enumerate([opposite, across]):
                for c in range(cuts):
                    b_copy(r, c, 2 + k, partner).wait_recv()
                    b_copy(r, c, 2 + k, partner).start()
            for c in range(cuts):
                b_copy(partner, c, 0, partner).wait_recv()
            for c in range(cuts):
                mid_direct(c).wait_send()
                for k in range(2):
                    mid_relay(k, c).wait_send()
                    b_copy([opposite, across][k], c, 2 + k, partner).wait_send()

        @pl.when(is_end)
        def _():
            for r in [partner, across, opposite]:
                for c in range(cuts):
                    b_copy(r, c, 0, partner).wait_recv()
            for c in range(cuts):
                for k in range(3):
                    end_a(k, c).wait_send()

    else:
        for c in range(cuts):
            for d in range(1, copies):
                b_copy(lax.rem(me_r + d, copies), c, 0, partner).wait_recv()
                far(d, c).wait_send()
    for c in range(cuts):
        for copy in own_sends(c):
            copy.wait_send()
    for d in range(1, shards):
        to = lax.rem(me_s + d, shards)
        a2_copy(to).wait_send()
        b1_copy(to).wait_send()


def place(shards, copies, table, got, *refs):
    stats, direction, outs, sem = refs[:4], refs[4], refs[5:9], refs[9]
    others = [
        pltpu.make_async_copy(src, dst, sem.at[1 + k])
        for k, (src, dst) in enumerate(zip(stats, outs))
    ]
    for copy in others:
        copy.start()

    def put(k, carry):
        block = table[lax.rem(k, shards) * copies + k // shards]
        pltpu.make_async_copy(got.at[k], direction.at[block], sem.at[0]).start()
        return carry

    lax.fori_loop(0, shards * copies, put, 0, unroll=8)
    pltpu.make_async_copy(got, direction, sem.at[0]).wait()
    for copy in others:
        copy.wait()


def local(shards, copies, grads, table, *factors):
    blocks, rows, order = grads.shape[1:]
    cuts = 2
    vmem = pl.BlockSpec(memory_space=pltpu.VMEM)
    smem = pl.BlockSpec(memory_space=pltpu.SMEM)
    hbm = pl.BlockSpec(memory_space=pltpu.HBM)
    code = jax.ShapeDtypeStruct((1, order, order), BF16)
    scale = jax.ShapeDtypeStruct((1, order // QG, order), F32)
    outs = [jax.ShapeDtypeStruct((blocks, rows, order), BF16), code, scale, code, scale]
    dma = pltpu.SemaphoreType.DMA
    results = pl.pallas_call(
        functools.partial(kernel, shards, copies, cuts),
        out_shape=outs,
        in_specs=[smem] + [hbm] * 9,
        out_specs=[vmem] * 5,
        scratch_shapes=[pltpu.VMEM((blocks, rows, order), BF16)]
        + [pltpu.VMEM(f.shape, f.dtype) for f in factors]
        + [
            pltpu.VMEM((blocks, rows, order), BF16),
            pltpu.VMEM((max(4, copies - 1), shards, rows, order), BF16),
            pltpu.VMEM((shards, rows, order), BF16),
            pltpu.VMEM((shards, rows, order), BF16),
            pltpu.VMEM((shards, rows, order), BF16),
            dma((9,)),
            dma((copies, cuts)),
            dma((copies, cuts)),
            dma((shards,)),
            dma((shards,)),
            dma((shards,)),
            dma((shards,)),
            dma((copies, cuts)),
            dma((copies, cuts)),
        ],
        compiler_params=pltpu.CompilerParams(
            collective_id=0, has_side_effects=True, vmem_limit_bytes=VMEM_BYTES
        ),
    )(table, grads, *factors)
    return pl.pallas_call(
        functools.partial(place, shards, copies),
        out_shape=outs,
        in_specs=[smem] + [hbm] * 5,
        out_specs=[hbm] * 5,
        scratch_shapes=[dma((5,))],
        compiler_params=pltpu.CompilerParams(vmem_limit_bytes=VMEM_BYTES),
    )(table, *results)


def solution(mesh):
    slots = P(("shard", "replica"), None, None)
    return jax.shard_map(
        functools.partial(local, mesh.shape["shard"], mesh.shape["replica"]),
        mesh=mesh,
        in_specs=(P("replica", None, "shard", None), P()) + (slots,) * 8,
        out_specs=(P(None, "shard", None), slots, slots, slots, slots),
        check_vma=False,
    )
```

```python
import functools

import jax
import jax.numpy as jnp
from jax import lax
from jax.experimental import pallas as pl
from jax.experimental.pallas import tpu as pltpu
from jax.sharding import PartitionSpec as P

QG = 128
DECAY = 0.9
EPSILON = 1e-06
VMEM_BYTES = 64 * 1024 * 1024
MESH = pl.DeviceIdType.MESH
F32 = jnp.float32
BF16 = jnp.bfloat16


def kernel(
    shards,
    copies,
    cuts,
    table,
    grads_hbm,
    lc_hbm,
    ls_hbm,
    rc_hbm,
    rs_hbm,
    lrc_hbm,
    lrs_hbm,
    rrc_hbm,
    rrs_hbm,
    got,
    new_left,
    new_left_scale,
    new_right,
    new_right_scale,
    grads,
    lc,
    ls,
    rc,
    rs,
    lrc,
    lrs,
    rrc,
    rrs,
    packed,
    relayed,
    pieces,
    moved,
    in_sem,
    relay_send,
    relay_recv,
    a_send,
    a_recv,
    b_send,
    b_recv,
    f_send,
):
    me_s = lax.axis_index("shard")
    me_r = lax.axis_index("replica")
    rows = grads.shape[1]
    order = lc.shape[1]
    blocks = shards * copies
    size = shards // cuts
    in_line = copies == 4

    loads = []
    for k, (src, dst) in enumerate(
        [
            (grads_hbm.at[0], grads),
            (lrc_hbm, lrc),
            (lrs_hbm, lrs),
            (rrc_hbm, rrc),
            (rrs_hbm, rrs),
            (lc_hbm, lc),
            (ls_hbm, ls),
            (rc_hbm, rc),
            (rs_hbm, rs),
        ]
    ):
        copy = pltpu.make_async_copy(src, dst, in_sem.at[k])
        copy.start()
        loads.append(copy)

    def device(k):
        return (lax.rem(k, shards), k // shards)

    me = me_r * shards + me_s
    barrier = pltpu.get_barrier_semaphore()

    def greet(d, carry):
        pl.semaphore_signal(
            barrier, inc=1, device_id=device(lax.rem(me + d, blocks)), device_id_type=MESH
        )
        return carry

    lax.fori_loop(1, blocks, greet, 0, unroll=True if in_line else 1)

    loads[0].wait()

    def pack(k, carry):
        packed[k] = grads[table[lax.rem(k, shards) * copies + k // shards]]
        return carry

    lax.fori_loop(0, blocks, pack, 0, unroll=8)
    pl.semaphore_wait(barrier, blocks - 1)

    partner = me_r + 1 - 2 * lax.rem(me_r, 2)
    opposite = copies - 1 - me_r
    across = copies - 1 - partner
    is_end = jnp.logical_or(me_r == 0, me_r == copies - 1)
    is_mid = jnp.logical_not(is_end)
    kinds = pieces.shape[0]

    def group(r, c):
        return pl.ds(r * shards + c * size, size)

    def a_copy(src, kind, k, to_s, to_r):
        return pltpu.make_async_remote_copy(
            src_ref=src,
            dst_ref=pieces.at[kind, me_s],
            send_sem=a_send.at[k, to_s],
            recv_sem=a_recv.at[kind, me_s],
            device_id=(to_s, to_r),
            device_id_type=MESH,
        )

    def own_a(k, to_s, to_r, kind):
        return a_copy(packed.at[to_r * shards + to_s], kind, k, to_s, to_r)

    def a_arrival(kind, source):
        return pltpu.make_async_remote_copy(
            src_ref=packed.at[source],
            dst_ref=pieces.at[kind, source],
            send_sem=a_send.at[0, source],
            recv_sem=a_recv.at[kind, source],
            device_id=(source, partner if in_line else lax.rem(me_r + 1, copies)),
            device_id_type=MESH,
        )

    def relay_copy(k, c):
        return pltpu.make_async_remote_copy(
            src_ref=packed.at[group([across, opposite][k], c)],
            dst_ref=relayed.at[k, pl.ds(c * size, size)],
            send_sem=relay_send.at[k, c],
            recv_sem=relay_recv.at[k, c],
            device_id=(me_s, partner),
            device_id_type=MESH,
        )

    def pair_a(k, to_s):
        return a_copy(relayed.at[k, to_s], 2, 2 + k, to_s, [opposite, across][k])

    def relay(k):
        for c in range(cuts):
            relay_copy(k, c).wait_recv()
            at = pl.ds(c * size, size)
            own = packed[group([opposite, across][k], c)].astype(F32)
            relayed[k, at] = (relayed[k, at].astype(F32) + own).astype(BF16)
            for n in range(size):
                pair_a(k, c * size + lax.rem(me_s + n, size)).start()

    around = [lax.rem(me_s + d, shards) for d in range(shards)]
    OWN, DIRECT = 0, 1

    if in_line:

        @pl.when(is_end)
        def _():
            for c in range(cuts):
                relay_copy(0, c).start()
            for s in around:
                own_a(1, s, partner, DIRECT).start()
            for c in range(cuts):
                relay_copy(1, c).start()
            for s in around[1:]:
                own_a(0, s, me_r, OWN).start()

        @pl.when(is_mid)
        def _():
            for s in around[1:]:
                own_a(0, s, me_r, OWN).start()
            for s in around:
                own_a(1, s, partner, DIRECT).start()
            relay(0)

        pieces[OWN, me_s] = packed[me]
    else:

        def all_a(d, act):
            to_s, to_r = device(lax.rem(me + d, blocks))
            act(own_a(to_r, to_s, to_r, me_r))

        def start_a(d, carry):
            all_a(d, lambda copy: copy.start())
            return carry

        lax.fori_loop(1, blocks, start_a, 0)
        pieces[me_r, me_s] = packed[me]

    for copy in loads[1:]:
        copy.wait()
    zeros = jnp.zeros((2, order), F32)
    columns = jnp.concatenate([ls[0], rs[0], lrs[0], zeros], axis=0).T

    if in_line:
        for s in around[1:]:
            a_arrival(OWN, s).wait_recv()
        for kind in (1, 2):
            for s in around:
                a_arrival(kind, s).wait_recv()
    else:

        def await_a(d, carry):
            source, kind = device(lax.rem(me + d, blocks))
            a_arrival(kind, source).wait_recv()
            return carry

        lax.fori_loop(1, blocks, await_a, 0)

    summed32 = pieces[0].astype(F32)
    for kind in range(1, kinds):
        summed32 = summed32 + pieces[kind].astype(F32)
    summed32 = summed32.reshape(order, order)
    summed = summed32.astype(BF16)
    half = columns[:, 4:5] * jnp.dot(lrc[0, :, :QG], summed[:QG], preferred_element_type=F32)
    half = half + columns[:, 5:6] * jnp.dot(
        lrc[0, :, QG:], summed[QG:], preferred_element_type=F32
    )
    product = jnp.concatenate(
        [
            jnp.dot(
                (half * rrs[0, g : g + 1]).astype(BF16),
                rrc[0, :, g * QG : (g + 1) * QG],
                preferred_element_type=F32,
            )
            for g in range(order // QG)
        ],
        axis=1,
    )
    count = 1.0 / (order * order)
    grad_power = jnp.sum(jnp.sum(summed32 * summed32, axis=0, keepdims=True), axis=1, keepdims=True)
    prod_power = jnp.sum(jnp.sum(product * product, axis=0, keepdims=True), axis=1, keepdims=True)
    ratio = jnp.sqrt(grad_power * count + EPSILON) / jnp.sqrt(prod_power * count + EPSILON)
    moved[...] = (product * ratio).reshape(shards, rows, order).astype(BF16)

    def b_copy(k, to_s, to_r):
        return pltpu.make_async_remote_copy(
            src_ref=moved.at[to_s],
            dst_ref=got.at[me],
            send_sem=b_send.at[k, to_s],
            recv_sem=b_recv.at[me],
            device_id=(to_s, to_r),
            device_id_type=MESH,
        )

    def forward(k, s):
        at = [opposite, across][k] * shards + s
        return pltpu.make_async_remote_copy(
            src_ref=got.at[at],
            dst_ref=got.at[at],
            send_sem=f_send.at[k, s],
            recv_sem=b_recv.at[at],
            device_id=(me_s, partner),
            device_id_type=MESH,
        )

    def b_arrival(r, s):
        at = r * shards + s
        return pltpu.make_async_remote_copy(
            src_ref=got.at[at],
            dst_ref=got.at[at],
            send_sem=b_send.at[0, s],
            recv_sem=b_recv.at[at],
            device_id=(me_s, partner if in_line else lax.rem(me_r + 1, copies)),
            device_id_type=MESH,
        )

    if in_line:

        @pl.when(is_end)
        def _():
            for s in around:
                b_copy(2, s, across).start()
            for d, s in enumerate(around):
                b_copy(1, s, partner).start()
                if d:
                    b_copy(0, s, me_r).start()

        @pl.when(is_mid)
        def _():
            for s in around:
                b_copy(1, s, partner).start()
            relay(1)
            for d, s in enumerate(around):
                b_copy(2, s, opposite).start()
                if d:
                    b_copy(0, s, me_r).start()

    else:

        def start_b(d, carry):
            to_s, to_r = device(lax.rem(me + d, blocks))
            b_copy(to_r, to_s, to_r).start()
            return carry

        lax.fori_loop(1, blocks, start_b, 0)
    got[me] = moved[me_s]

    lane = lax.broadcasted_iota(jnp.int32, (order, QG), 1)

    def statistic(k, code, contracted, out, steps):
        gram = lax.dot_general(
            summed, summed, (((contracted,), (contracted,)), ((), ())), preferred_element_type=F32
        )
        for g in range(order // QG):
            at = 2 * k + g
            cols = slice(g * QG, (g + 1) * QG)
            old = code[0, :, cols].astype(F32) * columns[:, at : at + 1]
            new = DECAY * old + (1.0 - DECAY) * gram[:, cols]
            step = (jnp.max(jnp.abs(new), axis=1, keepdims=True) + EPSILON) / 7.0
            out[0, :, cols] = (new * (1.0 / step)).astype(BF16)
            steps = jnp.where(lane == at, step, steps)
        return steps

    steps = statistic(0, lc, 1, new_left, jnp.zeros((order, QG), F32))

    steps = statistic(1, rc, 0, new_right, steps)
    flipped = steps.T
    new_left_scale[0] = flipped[0:2]
    new_right_scale[0] = flipped[2:4]

    if in_line:

        @pl.when(is_mid)
        def _():
            for k, r in enumerate([opposite, across]):
                for s in around:
                    b_arrival(r, s).wait_recv()
                    forward(k, s).start()
            for s in around:
                own_a(1, s, partner, DIRECT).wait_send()
                b_copy(1, s, partner).wait_send()
                b_copy(2, s, opposite).wait_send()
                for k in range(2):
                    pair_a(k, s).wait_send()
                    forward(k, s).wait_send()

        @pl.when(is_end)
        def _():
            for r in (opposite, across):
                for s in around:
                    b_arrival(r, s).wait_recv()
            for s in around:
                own_a(1, s, partner, DIRECT).wait_send()
                b_copy(1, s, partner).wait_send()
                b_copy(2, s, across).wait_send()
            for k in range(2):
                for c in range(cuts):
                    relay_copy(k, c).wait_send()

        for s in around:
            b_arrival(partner, s).wait_recv()
        for s in around[1:]:
            b_arrival(me_r, s).wait_recv()
            own_a(0, s, me_r, OWN).wait_send()
            b_copy(0, s, me_r).wait_send()
    else:

        def finish(d, carry):
            to_s, to_r = device(lax.rem(me + d, blocks))
            b_arrival(to_r, to_s).wait_recv()
            all_a(d, lambda copy: copy.wait_send())
            b_copy(to_r, to_s, to_r).wait_send()
            return carry

        lax.fori_loop(1, blocks, finish, 0)


def place(shards, copies, table, got, *refs):
    stats, direction, outs, sem = refs[:4], refs[4], refs[5:9], refs[9]
    others = [
        pltpu.make_async_copy(src, dst, sem.at[1 + k])
        for k, (src, dst) in enumerate(zip(stats, outs))
    ]
    for copy in others:
        copy.start()

    def put(k, carry):
        block = table[lax.rem(k, shards) * copies + k // shards]
        pltpu.make_async_copy(got.at[k], direction.at[block], sem.at[0]).start()
        return carry

    lax.fori_loop(0, shards * copies, put, 0, unroll=8)
    pltpu.make_async_copy(got, direction, sem.at[0]).wait()
    for copy in others:
        copy.wait()


def local(shards, copies, grads, table, *factors):
    blocks, rows, order = grads.shape[1:]
    cuts = 4
    vmem = pl.BlockSpec(memory_space=pltpu.VMEM)
    smem = pl.BlockSpec(memory_space=pltpu.SMEM)
    hbm = pl.BlockSpec(memory_space=pltpu.HBM)
    code = jax.ShapeDtypeStruct((1, order, order), BF16)
    scale = jax.ShapeDtypeStruct((1, order // QG, order), F32)
    outs = [jax.ShapeDtypeStruct((blocks, rows, order), BF16), code, scale, code, scale]
    dma = pltpu.SemaphoreType.DMA
    results = pl.pallas_call(
        functools.partial(kernel, shards, copies, cuts),
        out_shape=outs,
        in_specs=[smem] + [hbm] * 9,
        out_specs=[vmem] * 5,
        scratch_shapes=[pltpu.VMEM((blocks, rows, order), BF16)]
        + [pltpu.VMEM(f.shape, f.dtype) for f in factors]
        + [
            pltpu.VMEM((blocks, rows, order), BF16),
            pltpu.VMEM((2, shards, rows, order), BF16),
            pltpu.VMEM((3 if copies == 4 else copies, shards, rows, order), BF16),
            pltpu.VMEM((shards, rows, order), BF16),
            dma((9,)),
            dma((2, cuts)),
            dma((2, cuts)),
            dma((copies, shards)),
            dma((copies, shards)),
            dma((copies, shards)),
            dma((blocks,)),
            dma((2, shards)),
        ],
        compiler_params=pltpu.CompilerParams(
            collective_id=0, has_side_effects=True, vmem_limit_bytes=VMEM_BYTES
        ),
    )(table, grads, *factors)
    return pl.pallas_call(
        functools.partial(place, shards, copies),
        out_shape=outs,
        in_specs=[smem] + [vmem] * 5,
        out_specs=[hbm] * 5,
        scratch_shapes=[dma((5,))],
        compiler_params=pltpu.CompilerParams(vmem_limit_bytes=VMEM_BYTES),
    )(table, *results)


def solution(mesh):
    slots = P(("shard", "replica"), None, None)
    return jax.shard_map(
        functools.partial(local, mesh.shape["shard"], mesh.shape["replica"]),
        mesh=mesh,
        in_specs=(P("replica", None, "shard", None), P()) + (slots,) * 8,
        out_specs=(P(None, "shard", None), slots, slots, slots, slots),
        check_vma=False,
    )
```

```python
import functools

import jax
import jax.numpy as jnp
from jax import lax
from jax.experimental import pallas as pl
from jax.experimental.pallas import tpu as pltpu
from jax.sharding import PartitionSpec as P

QG = 128
DECAY = 0.9
EPSILON = 1e-06
VMEM_BYTES = 64 * 1024 * 1024
MESH = pl.DeviceIdType.MESH
F32 = jnp.float32
BF16 = jnp.bfloat16


def kernel(
    shards,
    copies,
    cuts,
    table,
    grads_hbm,
    lc_hbm,
    ls_hbm,
    rc_hbm,
    rs_hbm,
    lrc_hbm,
    lrs_hbm,
    rrc_hbm,
    rrs_hbm,
    got_hbm,
    new_left_hbm,
    new_left_scale_hbm,
    new_right_hbm,
    new_right_scale_hbm,
    grads,
    lc,
    ls,
    rc,
    rs,
    lrc,
    lrs,
    rrc,
    rrs,
    packed,
    relayed,
    pieces,
    moved,
    got,
    new_left,
    new_left_scale,
    new_right,
    new_right_scale,
    in_sem,
    out_sem,
    relay_send,
    relay_recv,
    a_send,
    a_recv,
    b_send,
    b_recv,
    f_send,
):
    me_s = lax.axis_index("shard")
    me_r = lax.axis_index("replica")
    rows = grads.shape[1]
    order = lc.shape[1]
    blocks = shards * copies
    size = shards // cuts
    in_line = copies == 4

    loads = []
    for k, (src, dst) in enumerate(
        [
            (grads_hbm.at[0], grads),
            (lrc_hbm, lrc),
            (lrs_hbm, lrs),
            (rrc_hbm, rrc),
            (rrs_hbm, rrs),
            (lc_hbm, lc),
            (ls_hbm, ls),
            (rc_hbm, rc),
            (rs_hbm, rs),
        ]
    ):
        copy = pltpu.make_async_copy(src, dst, in_sem.at[k])
        copy.start()
        loads.append(copy)

    def device(k):
        return (lax.rem(k, shards), k // shards)

    me = me_r * shards + me_s
    barrier = pltpu.get_barrier_semaphore()

    def greet(d, carry):
        pl.semaphore_signal(
            barrier, inc=1, device_id=device(lax.rem(me + d, blocks)), device_id_type=MESH
        )
        return carry

    lax.fori_loop(1, blocks, greet, 0, unroll=True if in_line else 1)

    loads[0].wait()

    def pack(k, carry):
        packed[k] = grads[table[lax.rem(k, shards) * copies + k // shards]]
        return carry

    lax.fori_loop(0, blocks, pack, 0, unroll=8)
    pl.semaphore_wait(barrier, blocks - 1)

    partner = me_r + 1 - 2 * lax.rem(me_r, 2)
    opposite = copies - 1 - me_r
    across = copies - 1 - partner
    is_end = jnp.logical_or(me_r == 0, me_r == copies - 1)
    is_mid = jnp.logical_not(is_end)
    kinds = pieces.shape[0]

    def group(r, c):
        return pl.ds(r * shards + c * size, size)

    def a_copy(src, kind, k, to_s, to_r):
        return pltpu.make_async_remote_copy(
            src_ref=src,
            dst_ref=pieces.at[kind, me_s],
            send_sem=a_send.at[k, to_s],
            recv_sem=a_recv.at[kind, me_s],
            device_id=(to_s, to_r),
            device_id_type=MESH,
        )

    def own_a(k, to_s, to_r, kind):
        return a_copy(packed.at[to_r * shards + to_s], kind, k, to_s, to_r)

    def a_arrival(kind, source):
        return pltpu.make_async_remote_copy(
            src_ref=packed.at[source],
            dst_ref=pieces.at[kind, source],
            send_sem=a_send.at[0, source],
            recv_sem=a_recv.at[kind, source],
            device_id=(source, partner if in_line else lax.rem(me_r + 1, copies)),
            device_id_type=MESH,
        )

    def relay_copy(k, c):
        return pltpu.make_async_remote_copy(
            src_ref=packed.at[group([across, opposite][k], c)],
            dst_ref=relayed.at[k, pl.ds(c * size, size)],
            send_sem=relay_send.at[k, c],
            recv_sem=relay_recv.at[k, c],
            device_id=(me_s, partner),
            device_id_type=MESH,
        )

    def pair_a(k, to_s):
        return a_copy(relayed.at[k, to_s], 2, 2 + k, to_s, [opposite, across][k])

    def relay(k):
        for c in range(cuts):
            relay_copy(k, c).wait_recv()
            at = pl.ds(c * size, size)
            own = packed[group([opposite, across][k], c)].astype(F32)
            relayed[k, at] = (relayed[k, at].astype(F32) + own).astype(BF16)
            for n in range(size):
                pair_a(k, c * size + lax.rem(me_s + n, size)).start()

    around = [lax.rem(me_s + d, shards) for d in range(shards)]
    OWN, DIRECT = 0, 1

    if in_line:

        @pl.when(is_end)
        def _():
            for c in range(cuts):
                relay_copy(0, c).start()
            for s in around:
                own_a(1, s, partner, DIRECT).start()
            for c in range(cuts):
                relay_copy(1, c).start()
            for s in around[1:]:
                own_a(0, s, me_r, OWN).start()

        @pl.when(is_mid)
        def _():
            for s in around[1:]:
                own_a(0, s, me_r, OWN).start()
            relay(0)
            for s in around:
                own_a(1, s, partner, DIRECT).start()

        pieces[OWN, me_s] = packed[me]
    else:

        def all_a(d, act):
            to_s, to_r = device(lax.rem(me + d, blocks))
            act(own_a(to_r, to_s, to_r, me_r))

        def start_a(d, carry):
            all_a(d, lambda copy: copy.start())
            return carry

        lax.fori_loop(1, blocks, start_a, 0)
        pieces[me_r, me_s] = packed[me]

    for copy in loads[1:]:
        copy.wait()
    zeros = jnp.zeros((2, order), F32)
    columns = jnp.concatenate([ls[0], rs[0], lrs[0], zeros], axis=0).T

    if in_line:
        for s in around[1:]:
            a_arrival(OWN, s).wait_recv()
        for kind in (1, 2):
            for s in around:
                a_arrival(kind, s).wait_recv()
    else:

        def await_a(d, carry):
            source, kind = device(lax.rem(me + d, blocks))
            a_arrival(kind, source).wait_recv()
            return carry

        lax.fori_loop(1, blocks, await_a, 0)

    summed32 = pieces[0].astype(F32)
    for kind in range(1, kinds):
        summed32 = summed32 + pieces[kind].astype(F32)
    summed32 = summed32.reshape(order, order)
    summed = summed32.astype(BF16)
    half = columns[:, 4:5] * jnp.dot(lrc[0, :, :QG], summed[:QG], preferred_element_type=F32)
    half = half + columns[:, 5:6] * jnp.dot(
        lrc[0, :, QG:], summed[QG:], preferred_element_type=F32
    )
    product = jnp.concatenate(
        [
            jnp.dot(
                (half * rrs[0, g : g + 1]).astype(BF16),
                rrc[0, :, g * QG : (g + 1) * QG],
                preferred_element_type=F32,
            )
            for g in range(order // QG)
        ],
        axis=1,
    )
    count = 1.0 / (order * order)
    grad_power = jnp.sum(jnp.sum(summed32 * summed32, axis=0, keepdims=True), axis=1, keepdims=True)
    prod_power = jnp.sum(jnp.sum(product * product, axis=0, keepdims=True), axis=1, keepdims=True)
    ratio = jnp.sqrt(grad_power * count + EPSILON) / jnp.sqrt(prod_power * count + EPSILON)
    moved[...] = (product * ratio).reshape(shards, rows, order).astype(BF16)

    def b_copy(k, to_s, to_r):
        return pltpu.make_async_remote_copy(
            src_ref=moved.at[to_s],
            dst_ref=got.at[me],
            send_sem=b_send.at[k, to_s],
            recv_sem=b_recv.at[me],
            device_id=(to_s, to_r),
            device_id_type=MESH,
        )

    def forward(k, s):
        at = [opposite, across][k] * shards + s
        return pltpu.make_async_remote_copy(
            src_ref=got.at[at],
            dst_ref=got.at[at],
            send_sem=f_send.at[k, s],
            recv_sem=b_recv.at[at],
            device_id=(me_s, partner),
            device_id_type=MESH,
        )

    def b_arrival(r, s):
        at = r * shards + s
        return pltpu.make_async_remote_copy(
            src_ref=got.at[at],
            dst_ref=got.at[at],
            send_sem=b_send.at[0, s],
            recv_sem=b_recv.at[at],
            device_id=(me_s, partner if in_line else lax.rem(me_r + 1, copies)),
            device_id_type=MESH,
        )

    if in_line:

        @pl.when(is_end)
        def _():
            for s in around:
                b_copy(2, s, across).start()
            for s in around:
                b_copy(1, s, partner).start()
            for s in around[1:]:
                b_copy(0, s, me_r).start()

        @pl.when(is_mid)
        def _():
            relay(1)
            for s in around:
                b_copy(2, s, opposite).start()
            for d, s in enumerate(around):
                b_copy(1, s, partner).start()
                if d:
                    b_copy(0, s, me_r).start()

    else:

        def start_b(d, carry):
            to_s, to_r = device(lax.rem(me + d, blocks))
            b_copy(to_r, to_s, to_r).start()
            return carry

        lax.fori_loop(1, blocks, start_b, 0)
    got[me] = moved[me_s]

    lane = lax.broadcasted_iota(jnp.int32, (order, QG), 1)

    def statistic(k, code, contracted, out, steps):
        gram = lax.dot_general(
            summed, summed, (((contracted,), (contracted,)), ((), ())), preferred_element_type=F32
        )
        for g in range(order // QG):
            at = 2 * k + g
            cols = slice(g * QG, (g + 1) * QG)
            old = code[0, :, cols].astype(F32) * columns[:, at : at + 1]
            new = DECAY * old + (1.0 - DECAY) * gram[:, cols]
            step = (jnp.max(jnp.abs(new), axis=1, keepdims=True) + EPSILON) / 7.0
            out[0, :, cols] = (new * (1.0 / step)).astype(BF16)
            steps = jnp.where(lane == at, step, steps)
        return steps

    steps = statistic(0, lc, 1, new_left, jnp.zeros((order, QG), F32))

    steps = statistic(1, rc, 0, new_right, steps)
    flipped = steps.T
    new_left_scale[0] = flipped[0:2]
    new_right_scale[0] = flipped[2:4]
    stores = []
    for k, (src, dst) in enumerate(
        [
            (new_left, new_left_hbm),
            (new_left_scale, new_left_scale_hbm),
            (new_right, new_right_hbm),
            (new_right_scale, new_right_scale_hbm),
        ]
    ):
        copy = pltpu.make_async_copy(src, dst, out_sem.at[copies + k])
        copy.start()
        stores.append(copy)

    def store(r):
        at = pl.ds(r * shards, shards)
        return pltpu.make_async_copy(got.at[at], got_hbm.at[at], out_sem.at[r])


    if in_line:
        for s in around[1:]:
            b_arrival(me_r, s).wait_recv()
        store(me_r).start()

        @pl.when(is_mid)
        def _():
            for k, r in enumerate([opposite, across]):
                for s in around:
                    b_arrival(r, s).wait_recv()
                    forward(k, s).start()
                store(r).start()

        for s in around:
            b_arrival(partner, s).wait_recv()
        store(partner).start()

        @pl.when(is_end)
        def _():
            for r in (across, opposite):
                for s in around:
                    b_arrival(r, s).wait_recv()
                store(r).start()

        @pl.when(is_mid)
        def _():
            for s in around:
                own_a(1, s, partner, DIRECT).wait_send()
                b_copy(1, s, partner).wait_send()
                b_copy(2, s, opposite).wait_send()
                for k in range(2):
                    pair_a(k, s).wait_send()
                    forward(k, s).wait_send()

        @pl.when(is_end)
        def _():
            for s in around:
                own_a(1, s, partner, DIRECT).wait_send()
                b_copy(1, s, partner).wait_send()
                b_copy(2, s, across).wait_send()
            for k in range(2):
                for c in range(cuts):
                    relay_copy(k, c).wait_send()

        for s in around[1:]:
            own_a(0, s, me_r, OWN).wait_send()
            b_copy(0, s, me_r).wait_send()
    else:

        def finish(d, carry):
            to_s, to_r = device(lax.rem(me + d, blocks))
            b_arrival(to_r, to_s).wait_recv()
            all_a(d, lambda copy: copy.wait_send())
            b_copy(to_r, to_s, to_r).wait_send()
            return carry

        lax.fori_loop(1, blocks, finish, 0)
        for r in range(copies):
            store(r).start()
    for r in range(copies):
        store(r).wait()
    for copy in stores:
        copy.wait()


def place(shards, copies, table, got, *refs):
    stats, direction, outs, sem = refs[:4], refs[4], refs[5:9], refs[9]
    others = [
        pltpu.make_async_copy(src, dst, sem.at[1 + k])
        for k, (src, dst) in enumerate(zip(stats, outs))
    ]
    for copy in others:
        copy.start()

    def put(k, carry):
        block = table[lax.rem(k, shards) * copies + k // shards]
        pltpu.make_async_copy(got.at[k], direction.at[block], sem.at[0]).start()
        return carry

    lax.fori_loop(0, shards * copies, put, 0, unroll=8)
    pltpu.make_async_copy(got, direction, sem.at[0]).wait()
    for copy in others:
        copy.wait()


def local(shards, copies, grads, table, *factors):
    blocks, rows, order = grads.shape[1:]
    cuts = 4
    smem = pl.BlockSpec(memory_space=pltpu.SMEM)
    hbm = pl.BlockSpec(memory_space=pltpu.HBM)
    code = jax.ShapeDtypeStruct((1, order, order), BF16)
    scale = jax.ShapeDtypeStruct((1, order // QG, order), F32)
    outs = [jax.ShapeDtypeStruct((blocks, rows, order), BF16), code, scale, code, scale]
    dma = pltpu.SemaphoreType.DMA
    held = [pltpu.VMEM(o.shape, o.dtype) for o in outs]
    results = pl.pallas_call(
        functools.partial(kernel, shards, copies, cuts),
        out_shape=outs,
        in_specs=[smem] + [hbm] * 9,
        out_specs=[hbm] * 5,
        scratch_shapes=[pltpu.VMEM((blocks, rows, order), BF16)]
        + [pltpu.VMEM(f.shape, f.dtype) for f in factors]
        + [
            pltpu.VMEM((blocks, rows, order), BF16),
            pltpu.VMEM((2, shards, rows, order), BF16),
            pltpu.VMEM((3 if copies == 4 else copies, shards, rows, order), BF16),
            pltpu.VMEM((shards, rows, order), BF16),
        ]
        + held
        + [
            dma((9,)),
            dma((copies + 4,)),
            dma((2, cuts)),
            dma((2, cuts)),
            dma((copies, shards)),
            dma((copies, shards)),
            dma((copies, shards)),
            dma((blocks,)),
            dma((2, shards)),
        ],
        compiler_params=pltpu.CompilerParams(
            collective_id=0, has_side_effects=True, vmem_limit_bytes=VMEM_BYTES
        ),
    )(table, grads, *factors)
    return pl.pallas_call(
        functools.partial(place, shards, copies),
        out_shape=outs,
        in_specs=[smem] + [pl.BlockSpec(memory_space=pltpu.VMEM)] * 5,
        out_specs=[hbm] * 5,
        scratch_shapes=[dma((5,))],
        compiler_params=pltpu.CompilerParams(vmem_limit_bytes=VMEM_BYTES),
    )(table, *results)


def solution(mesh):
    slots = P(("shard", "replica"), None, None)
    return jax.shard_map(
        functools.partial(local, mesh.shape["shard"], mesh.shape["replica"]),
        mesh=mesh,
        in_specs=(P("replica", None, "shard", None), P()) + (slots,) * 8,
        out_specs=(P(None, "shard", None), slots, slots, slots, slots),
        check_vma=False,
    )
```
